32 devices in a mesh: grp: 4 (over z), wide: 8 (over y, x, core).
Axes of the slice: x: 2, y: 2, z: 4, core: 2. Of those that a mesh axis runs over, the one named last changes fastest.
Arguments:
- visibilities: bfloat16 [2, 8, 2048, 4096], P(None, None, 'wide', 'grp'), may hold values from -6 to 6
- filters: bfloat16 [4096, 64, 2048], P(('grp', 'wide')), may hold values from -0.125 to 0.125
- counts: int32 [4096], replicated, may hold values from 128 to 2048, as said below
- m_of_slot: int32 [4096], replicated, may hold values from 0 to 4095, each once
- band_of_block: int32 [4096, 8], replicated, may hold values from 0 to 1023
Outputs:
- kl_coeffs: bfloat16 [4096, 2, 8, 64], P(('grp', 'wide'))
- band_power: float32 [8, 1024], P(None, ('grp', 'wide'))
The draws below stay inside these ranges and needn't reach their ends.
Inputs may be any that keep to these rules, and one draw needn't show every extreme that they name: Mode m uses its first counts[m] baselines; both ends of the range are taken in every draw. `m_of_slot`: each m mode stands in exactly one slot.
All inputs are finite; a program needn't handle non-finite values.
Results may differ from the reference program's by a relative error of at most 0.0055.
Values may be sent and summed in bfloat16 or wider, within the bound.
A program may use at most 128 MiB of HBM per device.

```python
import math
import jax
import jax.numpy as jnp
from jax import lax

CH = 8
NB = 2048
NT = 4096
KL = 64
KB = 8
NBAND = 1024
NKB = 8


def draw_counts(key, part):
    modes = jnp.arange(NT, dtype=jnp.int32)
    lowest = NB // 16
    highest = NB - 7 * NB // 8 * modes // NT
    values = jax.random.randint(key, (NT,), lowest, highest + 1, dtype=jnp.int32)
    values = values.at[0].set(NB)
    values = values.at[NT - 1].set(lowest)
    return values


def place_ends(array, own_key, low, largest):
    longest = array.shape.index(max(array.shape))
    spots = []
    for shift in (0, 1):
        where = [jax.random.randint(jax.random.fold_in(own_key, axis), (), 0, length) for axis, length in enumerate(array.shape)]
        where[longest] = (where[longest] + shift) % array.shape[longest]
        spots.append(tuple(where))
    return array.at[spots[0]].set(low).at[spots[1]].set(largest)


def steps_of(key, shape, pieces, low, largest):
    gain, own = 1.0, jax.random.fold_in(key, 6)
    for position, shards_of in pieces:
        draws = jnp.exp(jax.random.uniform(jax.random.fold_in(own, position), (shards_of,), jnp.float32, low / len(pieces), largest / len(pieces)))
        gain = gain * jnp.repeat(draws, shape[position] // shards_of).reshape([-1 if axis == position else 1 for axis in range(len(shape))])
    return gain


def centred(rng, extent, deviation, reach, split=(), kind=jnp.bfloat16):
    factor_of = steps_of(rng, extent, split, -0.22, 0.18) if split else 1.0
    drawn = jax.random.normal(rng, extent, jnp.float32) * deviation * factor_of
    return jnp.minimum(jnp.maximum(drawn, -reach), reach).astype(kind)


def setup_inputs(seed: int = 0) -> dict:
    arg_keys = jax.random.split(jax.random.key(seed), 6)
    return {
        "visibilities": centred(arg_keys[0], (2, CH, NB, NT), 1.0, 6.0, ((2, 8), (3, 4))),
        "filters": centred(arg_keys[1], (NT, KL, NB), NB ** -0.5, 0.125, ((0, 32),)),
        "counts": draw_counts(jax.random.fold_in(arg_keys[5], 71), 0),
        "m_of_slot": jax.random.permutation(arg_keys[3], NT).astype(jnp.int32),
        "band_of_block": place_ends(jax.random.randint(arg_keys[4], (NT, NKB), 0, NBAND), jax.random.fold_in(arg_keys[4], 1), 0, NBAND - 1).astype(jnp.int32),
    }


def table_block(columns):
    times = jnp.arange(NT, dtype=jnp.int32)
    index = (times[:, None] * columns[None, :] % NT).astype(jnp.int32)
    angles = index.astype(jnp.float32) * (2.0 * math.pi / NT)
    return (jnp.cos(angles).astype(jnp.bfloat16), jnp.sin(angles).astype(jnp.bfloat16))

def reference(visibilities, filters, counts, m_of_slot, band_of_block):
    highest = lax.Precision.HIGHEST
    scale_dft = 1.0 / math.sqrt(NT)
    real_part = visibilities[0].reshape(CH * NB, NT).astype(jnp.float32)
    imag_part = visibilities[1].reshape(CH * NB, NT).astype(jnp.float32)
    mode_block = min(512, NT)

    def transform(columns):
        cos_table, sin_table = table_block(columns)
        cos_full = cos_table.astype(jnp.float32)
        sin_full = sin_table.astype(jnp.float32)
        spec_re = (jnp.dot(real_part, cos_full, precision=highest) + jnp.dot(imag_part, sin_full, precision=highest)) * scale_dft
        spec_im = (jnp.dot(imag_part, cos_full, precision=highest) - jnp.dot(real_part, sin_full, precision=highest)) * scale_dft
        return jnp.stack([spec_re, spec_im]).astype(jnp.bfloat16)
    blocks = lax.map(transform, m_of_slot.reshape(NT // mode_block, mode_block))
    spectrum = blocks.transpose(0, 3, 1, 2).reshape(NT, 2, CH, NB)
    slot_block = min(128, NT)
    slot_counts = counts[m_of_slot]

    def apply_filter(items):
        filter_rows, spec_rows, count_rows = items
        active = jnp.arange(NB, dtype=jnp.int32)[None, :] < count_rows[:, None]
        masked = jnp.where(active[:, None, None, :], spec_rows.astype(jnp.float32), 0.0)
        return jnp.einsum('sxcb,skb->sxck', masked, filter_rows.astype(jnp.float32), precision=highest)
    coeffs = lax.map(apply_filter, (filters.reshape(NT // slot_block, slot_block, KL, NB), spectrum.reshape(NT // slot_block, slot_block, 2, CH, NB), slot_counts.reshape(NT // slot_block, slot_block))).reshape(NT, 2, CH, KL)
    kl_coeffs = coeffs.astype(jnp.bfloat16)
    power = coeffs[:, 0] * coeffs[:, 0] + coeffs[:, 1] * coeffs[:, 1]
    block_power = power.reshape(NT, CH, NKB, KB).sum(axis=-1)
    band_ids = band_of_block[m_of_slot].reshape(-1)
    flat = block_power.transpose(0, 2, 1).reshape(NT * NKB, CH)
    sums = jax.ops.segment_sum(flat, band_ids, num_segments=NBAND)
    band_power = sums.T * (NBAND / (NT * KL))
    return (kl_coeffs, band_power)
```

```python
import math

import jax
import jax.numpy as jnp
import ml_dtypes
import numpy as np
from jax import lax
from jax.sharding import PartitionSpec as P


def factors(times):
    first = 1
    while first * first < times:
        first *= 2
    return first, times // first


def rotation(angles):
    cos, sin = np.cos(angles), np.sin(angles)
    return np.stack([np.stack([cos, sin]), np.stack([-sin, cos])]).astype(ml_dtypes.bfloat16)


def tables(times):
    n1, n2 = factors(times)
    one, two = np.arange(n1), np.arange(n2)
    first = rotation(2.0 * np.pi * (one[:, None] * one[None, :] % n1) / n1)
    modes = one[:, None, None] + n1 * two[None, :, None]
    second = rotation(2.0 * np.pi * (two[None, None, :] * modes % times) / times)
    return first, second


def body(visibilities, filters, counts, m_of_slot, band_of_block):
    highest = lax.Precision.HIGHEST
    channels = visibilities.shape[1]
    groups = lax.axis_size("grp")
    wides = lax.axis_size("wide")
    times = visibilities.shape[3] * groups
    slots, modes_kept, baselines = filters.shape
    blocks = band_of_block.shape[1]
    n1, n2 = factors(times)
    first, second = tables(times)
    local = lax.all_to_all(visibilities, "grp", split_axis=2, concat_axis=3, tiled=True)
    base_dev = local.shape[2]
    rows = channels * base_dev
    samples = local.reshape(2, rows, n1, n2)
    half = jnp.einsum("yxma,xrab->mbyr", first, samples, preferred_element_type=jnp.float32)
    half = (half * (1.0 / math.sqrt(times))).astype(jnp.bfloat16)
    spectrum = jnp.einsum("zymnb,mbyr->mnzr", second, half, preferred_element_type=jnp.float32)
    spectrum = spectrum.astype(jnp.bfloat16).reshape(times, 2 * rows)
    place_of_slot = (m_of_slot % n1) * n2 + m_of_slot // n1
    ordered = jnp.take(spectrum, place_of_slot, axis=0, mode="clip")
    ordered = ordered.reshape(groups * wides, slots, 2 * rows)
    moved = lax.all_to_all(ordered, ("grp", "wide"), split_axis=0, concat_axis=0, tiled=True)
    owned = moved.reshape(groups, wides, slots, 2, channels, base_dev).transpose(2, 3, 4, 1, 0, 5)
    owned = owned.reshape(slots, 2, channels, baselines)
    place = lax.axis_index(("grp", "wide"))
    mine = lax.dynamic_slice_in_dim(m_of_slot, place * slots, slots)
    active_counts = counts[mine]
    band_rows = band_of_block[mine]
    active = jnp.arange(baselines, dtype=jnp.int32)[None, :] < active_counts[:, None]
    masked = jnp.where(active[:, None, None, :], owned, jnp.zeros_like(owned))
    coeffs = jnp.einsum("sxcb,skb->sxck", masked, filters, preferred_element_type=jnp.float32)
    kl_coeffs = coeffs.astype(jnp.bfloat16)
    power = coeffs[:, 0] * coeffs[:, 0] + coeffs[:, 1] * coeffs[:, 1]
    block_power = power.reshape(slots, channels, blocks, modes_kept // blocks).sum(axis=-1)
    bands = BANDS
    one_hot = (band_rows[:, :, None] == jnp.arange(bands, dtype=jnp.int32)[None, None, :]).astype(
        jnp.float32
    )
    partial_sums = jnp.einsum("scj,sjn->cn", block_power, one_hot, precision=highest)
    band_scale = bands / (times * modes_kept)
    totals = lax.psum(partial_sums, ("grp", "wide"))
    band_dev = bands // (groups * wides)
    band_power = lax.dynamic_slice_in_dim(totals, place * band_dev, band_dev, 1) * band_scale
    return (kl_coeffs, band_power)


BANDS = 1024


def solution(mesh):
    placed = (P(None, None, "wide", "grp"), P(("grp", "wide"), None, None), P(), P(), P())
    return jax.shard_map(
        body,
        mesh=mesh,
        in_specs=placed,
        out_specs=(P(("grp", "wide"), None, None, None), P(None, ("grp", "wide"))),
        check_vma=False,
    )
```

```python
import math

import jax
import jax.numpy as jnp
import ml_dtypes
import numpy as np
from jax import lax
from jax.sharding import PartitionSpec as P


def factors(times):
    first = 1
    while first * first < times:
        first *= 2
    return first, times // first


def rotation(angles):
    cos, sin = np.cos(angles), np.sin(angles)
    return np.stack([np.stack([cos, sin]), np.stack([-sin, cos])]).astype(ml_dtypes.bfloat16)


def tables(times):
    n1, n2 = factors(times)
    one, two = np.arange(n1), np.arange(n2)
    first = rotation(2.0 * np.pi * (one[:, None] * one[None, :] % n1) / n1)
    modes = one[:, None, None] + n1 * two[None, :, None]
    second = rotation(2.0 * np.pi * (two[None, None, :] * modes % times) / times)
    return first, second


def body(visibilities, filters, counts, m_of_slot, band_of_block):
    highest = lax.Precision.HIGHEST
    channels = visibilities.shape[1]
    groups = lax.axis_size("grp")
    wides = lax.axis_size("wide")
    times = visibilities.shape[3] * groups
    slots, modes_kept, baselines = filters.shape
    blocks = band_of_block.shape[1]
    n1, n2 = factors(times)
    first, second = tables(times)
    ranks = groups * wides
    place_of_slot = (m_of_slot % n1) * n2 + m_of_slot // n1
    place = lax.axis_index(("grp", "wide"))
    mine = lax.dynamic_slice_in_dim(m_of_slot, place * slots, slots)
    active_counts = counts[mine]
    band_rows = band_of_block[mine]
    active = jnp.arange(baselines, dtype=jnp.int32)[None, :] < active_counts[:, None]
    masked = jnp.where(active[:, None, :], filters, jnp.zeros_like(filters))
    parts = 2 if channels % 2 == 0 else 1
    part = channels // parts
    regrouped = [
        lax.all_to_all(
            lax.slice_in_dim(visibilities, i * part, (i + 1) * part, axis=1),
            "grp", split_axis=2, concat_axis=3, tiled=True,
        )
        for i in range(parts)
    ]
    base_dev = regrouped[0].shape[2]
    rows = part * base_dev

    def transform(local):
        samples = local.reshape(2, rows, n1, n2)
        half = jnp.einsum("yxma,xrab->mbyr", first, samples, preferred_element_type=jnp.float32)
        half = (half * (1.0 / math.sqrt(times))).astype(jnp.bfloat16)
        spectrum = jnp.einsum("zymnb,mbyr->mnzr", second, half, preferred_element_type=jnp.float32)
        spectrum = spectrum.astype(jnp.bfloat16).reshape(times, 2 * rows)
        ordered = jnp.take(spectrum, place_of_slot, axis=0, mode="clip")
        return ordered.reshape(ranks, slots, 2 * rows)

    ordered = [transform(local) for local in regrouped]
    moved = [
        lax.all_to_all(one, ("grp", "wide"), split_axis=0, concat_axis=0, tiled=True)
        for one in ordered
    ]

    def filtered(one):
        owned = one.reshape(groups, wides, slots, 2, part, base_dev).transpose(2, 3, 4, 1, 0, 5)
        owned = owned.reshape(slots, 2, part, baselines)
        return jnp.einsum("sxcb,skb->sxck", owned, masked, preferred_element_type=jnp.float32)

    coeffs = jnp.concatenate([filtered(one) for one in moved], axis=2)
    kl_coeffs = coeffs.astype(jnp.bfloat16)
    power = coeffs[:, 0] * coeffs[:, 0] + coeffs[:, 1] * coeffs[:, 1]
    block_power = power.reshape(slots, channels, blocks, modes_kept // blocks).sum(axis=-1)
    bands = BANDS
    one_hot = (band_rows[:, :, None] == jnp.arange(bands, dtype=jnp.int32)[None, None, :]).astype(
        jnp.float32
    )
    partial_sums = jnp.einsum("scj,sjn->cn", block_power, one_hot, precision=highest)
    band_dev = bands // ranks
    slices = partial_sums.reshape(channels, ranks, band_dev).transpose(1, 0, 2)
    slices = lax.all_to_all(slices, ("grp", "wide"), split_axis=0, concat_axis=0, tiled=True)
    band_power = slices.sum(axis=0) * (bands / (times * modes_kept))
    return (kl_coeffs, band_power)


BANDS = 1024


def solution(mesh):
    placed = (P(None, None, "wide", "grp"), P(("grp", "wide"), None, None), P(), P(), P())
    return jax.shard_map(
        body,
        mesh=mesh,
        in_specs=placed,
        out_specs=(P(("grp", "wide"), None, None, None), P(None, ("grp", "wide"))),
        check_vma=False,
    )
```

```python
import math

import jax
import jax.numpy as jnp
import ml_dtypes
import numpy as np
from jax import lax
from jax.sharding import PartitionSpec as P


def factors(times):
    first = 1
    while first * first < times:
        first *= 2
    return first, times // first


def rotation(angles):
    cos, sin = np.cos(angles), np.sin(angles)
    return np.stack([np.stack([cos, sin]), np.stack([-sin, cos])]).astype(ml_dtypes.bfloat16)


def tables(times):
    n1, n2 = factors(times)
    one, two = np.arange(n1), np.arange(n2)
    first = rotation(2.0 * np.pi * (one[:, None] * one[None, :] % n1) / n1)
    modes = one[:, None, None] + n1 * two[None, :, None]
    second = rotation(2.0 * np.pi * (two[None, None, :] * modes % times) / times)
    return first, second


def body(visibilities, filters, counts, m_of_slot, band_of_block):
    highest = lax.Precision.HIGHEST
    channels = visibilities.shape[1]
    groups = lax.axis_size("grp")
    wides = lax.axis_size("wide")
    times = visibilities.shape[3] * groups
    slots, modes_kept, baselines = filters.shape
    blocks = band_of_block.shape[1]
    n1, n2 = factors(times)
    first, second = tables(times)
    ranks = groups * wides
    place_of_slot = (m_of_slot % n1) * n2 + m_of_slot // n1
    place = lax.axis_index(("grp", "wide"))
    mine = lax.dynamic_slice_in_dim(m_of_slot, place * slots, slots)
    active_counts = counts[mine]
    band_rows = band_of_block[mine]
    active = jnp.arange(baselines, dtype=jnp.int32)[None, :] < active_counts[:, None]
    masked = jnp.where(active[:, None, :], filters, jnp.zeros_like(filters))
    parts = 2 if channels % 2 == 0 else 1
    part = channels // parts
    regrouped = [
        lax.all_to_all(
            lax.slice_in_dim(visibilities, i * part, (i + 1) * part, axis=1),
            "grp", split_axis=2, concat_axis=3, tiled=True,
        )
        for i in range(parts)
    ]
    base_dev = regrouped[0].shape[2]
    rows = part * base_dev

    def transform(local):
        samples = local.reshape(2, rows, n1, n2)
        half = jnp.einsum("yxma,xrab->mbyr", first, samples, preferred_element_type=jnp.float32)
        half = (half * (1.0 / math.sqrt(times))).astype(jnp.bfloat16)
        spectrum = jnp.einsum("zymnb,mbyr->mnzr", second, half, preferred_element_type=jnp.float32)
        spectrum = spectrum.astype(jnp.bfloat16).reshape(times, 2 * rows)
        ordered = jnp.take(spectrum, place_of_slot, axis=0, mode="clip")
        return ordered.reshape(ranks, slots, 2 * rows)

    ordered = [transform(local) for local in regrouped]
    moved = [
        lax.all_to_all(one, ("grp", "wide"), split_axis=0, concat_axis=0, tiled=True)
        for one in ordered
    ]

    def filtered(one):
        owned = one.reshape(groups, wides, slots, 2, part, base_dev).transpose(2, 3, 4, 1, 0, 5)
        owned = owned.reshape(slots, 2, part, baselines)
        return jnp.einsum("sxcb,skb->sxck", owned, masked, preferred_element_type=jnp.float32)

    pieces = []
    for one in moved:
        if pieces:
            one, pieces[-1] = lax.optimization_barrier((one, pieces[-1]))
        pieces.append(filtered(one))
    coeffs = jnp.concatenate(pieces, axis=2)
    kl_coeffs = coeffs.astype(jnp.bfloat16)
    power = coeffs[:, 0] * coeffs[:, 0] + coeffs[:, 1] * coeffs[:, 1]
    block_power = power.reshape(slots, channels, blocks, modes_kept // blocks).sum(axis=-1)
    bands = BANDS
    one_hot = (band_rows[:, :, None] == jnp.arange(bands, dtype=jnp.int32)[None, None, :]).astype(
        jnp.float32
    )
    partial_sums = jnp.einsum("scj,sjn->cn", block_power, one_hot, precision=highest)
    band_dev = bands // ranks
    slices = partial_sums.reshape(channels, ranks, band_dev).transpose(1, 0, 2)
    slices = lax.all_to_all(slices, ("grp", "wide"), split_axis=0, concat_axis=0, tiled=True)
    band_power = slices.sum(axis=0) * (bands / (times * modes_kept))
    return (kl_coeffs, band_power)


BANDS = 1024


def solution(mesh):
    placed = (P(None, None, "wide", "grp"), P(("grp", "wide"), None, None), P(), P(), P())
    return jax.shard_map(
        body,
        mesh=mesh,
        in_specs=placed,
        out_specs=(P(("grp", "wide"), None, None, None), P(None, ("grp", "wide"))),
        check_vma=False,
    )
```

```python
import math

import jax
import jax.numpy as jnp
import ml_dtypes
import numpy as np
from jax import lax
from jax.sharding import PartitionSpec as P


def factors(times):
    first = 1
    while first * first < times:
        first *= 2
    return first, times // first


def rotation(angles):
    cos, sin = np.cos(angles), np.sin(angles)
    return np.stack([np.stack([cos, sin]), np.stack([-sin, cos])]).astype(ml_dtypes.bfloat16)


def tables(times):
    n1, n2 = factors(times)
    one, two = np.arange(n1), np.arange(n2)
    first = rotation(2.0 * np.pi * (one[:, None] * one[None, :] % n1) / n1)
    modes = one[:, None, None] + n1 * two[None, :, None]
    second = rotation(2.0 * np.pi * (two[None, None, :] * modes % times) / times)
    return first, second


def body(visibilities, filters, counts, m_of_slot, band_of_block):
    highest = lax.Precision.HIGHEST
    channels = visibilities.shape[1]
    groups = lax.axis_size("grp")
    wides = lax.axis_size("wide")
    times = visibilities.shape[3] * groups
    slots, modes_kept, baselines = filters.shape
    blocks = band_of_block.shape[1]
    n1, n2 = factors(times)
    first, second = tables(times)
    ranks = groups * wides
    place_of_slot = (m_of_slot % n1) * n2 + m_of_slot // n1
    place = lax.axis_index(("grp", "wide"))
    mine = lax.dynamic_slice_in_dim(m_of_slot, place * slots, slots)
    active_counts = counts[mine]
    band_rows = band_of_block[mine]
    active = jnp.arange(baselines, dtype=jnp.int32)[None, :] < active_counts[:, None]
    masked = jnp.where(active[:, None, :], filters, jnp.zeros_like(filters))
    parts = 2 if channels % 2 == 0 else 1
    part = channels // parts
    pieces, source = [], visibilities
    for i in range(parts):
        piece = lax.slice_in_dim(source, i * part, (i + 1) * part, axis=1)
        source, piece = lax.optimization_barrier((source, piece))
        pieces.append(piece)
    regrouped = [
        lax.all_to_all(piece, "grp", split_axis=2, concat_axis=3, tiled=True) for piece in pieces
    ]
    base_dev = regrouped[0].shape[2]
    rows = part * base_dev

    def transform(local):
        samples = local.reshape(2, rows, n1, n2)
        half = jnp.einsum("yxma,xrab->mbyr", first, samples, preferred_element_type=jnp.float32)
        half = (half * (1.0 / math.sqrt(times))).astype(jnp.bfloat16)
        spectrum = jnp.einsum("zymnb,mbyr->mnzr", second, half, preferred_element_type=jnp.float32)
        spectrum = spectrum.astype(jnp.bfloat16).reshape(times, 2 * rows)
        ordered = jnp.take(spectrum, place_of_slot, axis=0, mode="clip")
        return ordered.reshape(ranks, slots, 2 * rows)

    ordered = [transform(local) for local in regrouped]
    moved = [
        lax.all_to_all(one, ("grp", "wide"), split_axis=0, concat_axis=0, tiled=True)
        for one in ordered
    ]

    def filtered(one):
        owned = one.reshape(groups, wides, slots, 2, part, base_dev).transpose(2, 3, 4, 1, 0, 5)
        owned = owned.reshape(slots, 2, part, baselines)
        coeffs = jnp.einsum("sxcb,skb->sxck", owned, masked, preferred_element_type=jnp.float32)
        power = coeffs[:, 0] * coeffs[:, 0] + coeffs[:, 1] * coeffs[:, 1]
        block_power = power.reshape(slots, part, blocks, modes_kept // blocks).sum(axis=-1)
        sums = jnp.einsum("scj,sjn->cn", block_power, one_hot, precision=highest)
        return coeffs.astype(jnp.bfloat16), sums

    bands = BANDS
    one_hot = (band_rows[:, :, None] == jnp.arange(bands, dtype=jnp.int32)[None, None, :]).astype(
        jnp.float32
    )
    results = []
    for one in moved:
        if results:
            one, results[-1] = lax.optimization_barrier((one, results[-1]))
        results.append(filtered(one))
    kl_coeffs = jnp.concatenate([kept for kept, _ in results], axis=2)
    partial_sums = jnp.concatenate([sums for _, sums in results], axis=0)
    band_dev = bands // ranks
    slices = partial_sums.reshape(channels, ranks, band_dev).transpose(1, 0, 2)
    slices = lax.all_to_all(slices, ("grp", "wide"), split_axis=0, concat_axis=0, tiled=True)
    band_power = slices.sum(axis=0) * (bands / (times * modes_kept))
    return (kl_coeffs, band_power)


BANDS = 1024


def solution(mesh):
    placed = (P(None, None, "wide", "grp"), P(("grp", "wide"), None, None), P(), P(), P())
    return jax.shard_map(
        body,
        mesh=mesh,
        in_specs=placed,
        out_specs=(P(("grp", "wide"), None, None, None), P(None, ("grp", "wide"))),
        check_vma=False,
    )
```
